32 devices in a mesh: groups: 2 (over x), ptcl: 8 (over z, y), vol: 2 (over core).
Axes of the slice: x: 2, y: 2, z: 4, core: 2. Of those that a mesh axis runs over, the one named last changes fastest.
Arguments:
- reference_slabs: bfloat16 [8, 180, 5760], P('groups', 'vol'), parts along dimension 0, may hold values from -0.03125 to 0.03125
- slice_table: bfloat16 [128, 180], replicated, may hold values from -4 to 4
- images: bfloat16 [1536, 5760], P(('groups', 'ptcl'), 'vol'), parts along dimension 0, may hold values from -16 to 16
- offsets: float32 [1536, 16], P(('groups', 'ptcl')), parts along dimension 0, may hold values from -8 to 250
- orient_lists: int32 [1536, 16], P(('groups', 'ptcl')), parts along dimension 0, may hold values from 0 to 511
- counts: int32 [1536], P(('groups', 'ptcl')), parts along dimension 0, may hold values from 1 to 16, 6528 in all
Outputs:
- new_ref: bfloat16 [8, 180, 5760], P('groups', None, 'vol'), parts along dimension 0
- log_norm: float32 [1536], P(('groups', 'ptcl')), parts along dimension 0
The draws below stay inside these ranges and needn't reach their ends.
There are 2 independent parts, one for each index of `groups`. The reference program is written for one: setup_inputs(seed, part) draws one part's arguments, and reference() takes and returns one part's arrays. A program takes and returns all parts, laid end to end along the dimension named above; an argument that names none is the same for every part. Nothing has to cross between parts.
All inputs are finite; a program needn't handle non-finite values. No bound on the sum of `counts` on one device may be relied on, other than what follows from the above.
Results may differ from the reference program's by a relative error of at most 0.0079.
Values may be sent and summed in bfloat16 or wider, within the bound.
A program may use at most 128 MiB of HBM per device.

```python
import math
import jax
import jax.numpy as jnp
import numpy as np
from jax import lax

C = 4
KZ = 180
ORIENT = 128
K = 16
PIX = 5760
PTCL = 768


def slot_classes(key):
    light_key, head_key, rest_key, orient_key = jax.random.split(key, 4)
    faint_class = jax.random.randint(light_key, (), 0, C)
    head_class = (faint_class + 1 + jax.random.randint(head_key, (PTCL, 1), 0, C - 1)) % C
    rest_class = jax.random.randint(rest_key, (PTCL, K - 1), 0, C)
    classes = jnp.concatenate([head_class, rest_class], axis=1)
    orient_pick = jax.random.randint(orient_key, (PTCL, K), 0, ORIENT)
    return (classes * ORIENT + orient_pick, classes == faint_class)


def draw_orient_lists(key, part):
    pairs, faint_slots = slot_classes(key)
    return pairs.astype(jnp.int32)


def draw_offsets(key, part):
    pairs, faint_slots = slot_classes(key)
    key = jax.random.fold_in(key, 11)
    gap_key = jax.random.fold_in(key, 1)
    jitter_key = jax.random.fold_in(key, 2)
    relative = jnp.log(jnp.float32(0.0053 * ORIENT / PTCL)) - 0.18
    first_slot = jnp.arange(K, dtype=jnp.int32)[None, :] == 0
    lead_gap = jax.random.uniform(gap_key, (PTCL, 1), jnp.float32, 4.4, 5.4)
    jitter = jax.random.uniform(jitter_key, (PTCL, K), jnp.float32, -0.3, 0.3)
    shaped = jnp.where(first_slot, lead_gap, jnp.where(faint_slots, lead_gap + relative, jnp.float32(0.0)))
    return shaped + jitter


def level_of(stream_key, dims, cuts, smallest, largest):
    def one(position, shards_of):
        draws = jax.random.uniform(jax.random.fold_in(jax.random.fold_in(stream_key, 6), position), (shards_of,), jnp.float32, smallest / len(cuts), largest / len(cuts))
        return jnp.repeat(jnp.exp(draws), dims[position] // shards_of).reshape((-1,) + (1,) * (len(dims) - position - 1))

    loudness = one(*cuts[0])
    for cut in cuts[1:]:
        loudness = loudness * one(*cut)
    return loudness


def profile(number_of, total, most, lean):
    loads = [(1 << 20) // math.isqrt(rank ** lean) + 1 for rank in range(2, number_of + 1)]
    rest, given = total - most - (number_of - 1), [1] * (number_of - 1)
    while rest > 0:
        candidates = [i for i in range(number_of - 1) if given[i] < most]
        pool, remaining = sum([loads[i] for i in candidates]), rest
        for i in candidates:
            extra = min(most - given[i], max(1, remaining * loads[i] // pool), rest)
            given[i] = given[i] + extra
            rest = rest - extra
    return np.array([most] + given)


def ragged(rng, number_of, total, limit, skew):
    if number_of == 2:
        one = jax.random.randint(rng, (), max(1, total - limit), min(limit, total - 1) + 1)
        return jnp.stack([one, total - one])
    lengths = jnp.asarray(profile(number_of, total, limit, skew), jnp.int32)
    twos = (number_of - 1) // 2
    source_of, sink = lengths[1:1 + 2 * twos:2], lengths[2:2 + 2 * twos:2]
    margin = jnp.minimum(source_of - 1, limit - sink)
    moved = jax.random.randint(jax.random.fold_in(rng, 1), (twos,), 0, 1 << 20) % (margin + 1)
    lengths = lengths.at[1:1 + 2 * twos:2].set(source_of - moved).at[2:2 + 2 * twos:2].set(sink + moved)
    return lengths[jax.random.permutation(jax.random.fold_in(rng, 2), number_of)]


def scatter_about(stream_key, shape, deviation, most, pieces=(), kind=jnp.bfloat16):
    result = jax.random.normal(stream_key, shape, jnp.float32) * deviation
    if len(pieces) > 0:
        result = level_of(stream_key, shape, pieces, -0.22, 0.18) * result
    return jnp.clip(result, min=-most, max=most).astype(kind)


def setup_inputs(seed: int = 0, part: int = 0) -> dict:
    arg_keys = jax.random.split(jax.random.key(seed), 7)
    part_keys = jax.random.split(jax.random.fold_in(arg_keys[6], part), 7)
    return {
        "reference_slabs": scatter_about(part_keys[0], (C, KZ, PIX), (0.05 * KZ ** -0.5 * ORIENT ** 0.5 * 0.125), 0.03125, ((1, 2),)),
        "slice_table": scatter_about(arg_keys[1], (ORIENT, KZ), (8 * ORIENT ** -0.5), 4.0),
        "images": scatter_about(part_keys[2], (PTCL, PIX), 3.0, 16.0, ((0, 8), (1, 2))),
        "offsets": draw_offsets(jax.random.fold_in(jax.random.fold_in(arg_keys[6], part), 71), part),
        "orient_lists": draw_orient_lists(jax.random.fold_in(jax.random.fold_in(arg_keys[6], part), 71), part),
        "counts": ragged(part_keys[5], PTCL, PTCL * (K + 1) // 2, K, 1).astype(jnp.int32),
    }


def posterior(sel_cross, sel_power, offsets, counts, score_scale):
    scores = score_scale * (sel_cross - 0.5 * sel_power) + offsets
    slot_ids = jnp.arange(scores.shape[1], dtype=jnp.int32)
    live_slots = slot_ids[None, :] < counts[:, None]
    masked = jnp.where(live_slots, scores, jnp.float32(-1e+30))
    row_top = lax.optimization_barrier(jnp.max(masked, axis=1, keepdims=True))
    expon = jnp.where(live_slots, jnp.exp(masked - row_top), jnp.float32(0.0))
    row_total = lax.optimization_barrier(jnp.sum(expon, axis=1, keepdims=True))
    weights = expon / row_total
    log_norm = (row_top + jnp.log(row_total))[:, 0]
    return (weights, log_norm)

def spread_weights(weights, orient_lists, columns):
    targets = jnp.arange(columns, dtype=jnp.int32)
    spread_sum = jnp.zeros((weights.shape[0], columns), jnp.float32)
    for slot in range(weights.shape[1]):
        hits = (orient_lists[:, slot:slot + 1] == targets[None, :]).astype(jnp.float32)
        spread_sum = spread_sum + weights[:, slot:slot + 1] * hits
    return spread_sum.astype(jnp.bfloat16)

def reference(reference_slabs, slice_table, images, offsets, orient_lists, counts):
    highest = lax.Precision.HIGHEST
    columns = C * ORIENT
    kernel = slice_table.astype(jnp.float32)
    projection = jnp.einsum('ckp,ok->pco', reference_slabs.astype(jnp.float32), kernel, precision=highest)
    projection = projection.reshape(PIX, columns).astype(jnp.bfloat16)
    proj_wide = projection.astype(jnp.float32)
    powers = lax.optimization_barrier(jnp.sum(proj_wide * proj_wide, axis=0))
    crossed = jnp.dot(images, projection, preferred_element_type=jnp.float32)
    sel_cross = jnp.take_along_axis(crossed, orient_lists, axis=1)
    sel_power = powers[orient_lists]
    weights, log_norm = posterior(sel_cross, sel_power, offsets, counts, 4.0 / math.sqrt(PIX))
    spread = spread_weights(weights, orient_lists, columns)
    sum_rows = lax.dot_general(spread, images, (((0,), (0,)), ((), ())), preferred_element_type=jnp.float32).astype(jnp.bfloat16)
    totals = lax.optimization_barrier(jnp.sum(spread.astype(jnp.float32), axis=0))
    stacked = sum_rows.astype(jnp.float32).reshape(C, ORIENT, PIX)
    numerator = jnp.einsum('ok,cop->ckp', kernel, stacked, precision=highest)
    denominator = 1.0 + jnp.einsum('ok,co->ck', kernel * kernel, totals.reshape(C, ORIENT), precision=highest)
    new_ref = (numerator / denominator[:, :, None]).astype(jnp.bfloat16)
    return (new_ref, log_norm)
```

```python
import math

import jax
import jax.numpy as jnp
from jax import lax
from jax.sharding import PartitionSpec as P


def posterior(half_scores, offsets, counts, score_scale):
    scores = score_scale * half_scores + offsets
    slot_ids = jnp.arange(scores.shape[1], dtype=jnp.int32)
    live_slots = slot_ids[None, :] < counts[:, None]
    masked = jnp.where(live_slots, scores, jnp.float32(-1e30))
    row_top = jnp.max(masked, axis=1, keepdims=True)
    expon = jnp.where(live_slots, jnp.exp(masked - row_top), jnp.float32(0.0))
    row_total = jnp.sum(expon, axis=1, keepdims=True)
    weights = expon / row_total
    log_norm = (row_top + jnp.log(row_total))[:, 0]
    return (weights, log_norm)


def spread_weights(weights, orient_lists, columns):
    targets = jnp.arange(columns, dtype=jnp.int32)
    spread_sum = jnp.zeros((weights.shape[0], columns), jnp.float32)
    for slot in range(weights.shape[1]):
        hits = (orient_lists[:, slot : slot + 1] == targets[None, :]).astype(jnp.float32)
        spread_sum = spread_sum + weights[:, slot : slot + 1] * hits
    return spread_sum.astype(jnp.bfloat16)


def back_project(sum_rows, totals, slice_table, classes):
    orients = slice_table.shape[0]
    stacked = sum_rows.reshape(classes, orients, sum_rows.shape[1])
    numerator = jnp.einsum("ok,cop->ckp", slice_table, stacked, preferred_element_type=jnp.float32)
    kernel = slice_table.astype(jnp.float32)
    denominator = 1.0 + jnp.einsum(
        "ok,co->ck",
        kernel * kernel,
        totals.reshape(classes, orients),
        precision=lax.Precision.HIGHEST,
    )
    return (numerator / denominator[:, :, None]).astype(jnp.bfloat16)


def on_device(reference_slabs, slice_table, images, offsets, orient_lists, counts):
    classes, kz_dev, pixels = reference_slabs.shape
    orients = slice_table.shape[0]
    half_pixels = images.shape[1]
    columns = classes * orients
    halves = lax.axis_size("vol")
    vol = lax.axis_index("vol")
    all_images = lax.all_gather(images, "ptcl", axis=0, tiled=True)
    low, high = reference_slabs[:, :, :half_pixels], reference_slabs[:, :, half_pixels:]
    first = vol == 0
    mine = jnp.where(first, low, high)
    other = lax.ppermute(jnp.where(first, high, low), "vol", [(0, 1), (1, 0)])
    table_mine = jnp.where(first, slice_table[:, :kz_dev], slice_table[:, kz_dev:])
    table_other = jnp.where(first, slice_table[:, kz_dev:], slice_table[:, :kz_dev])
    projection = (
        jnp.einsum("ok,ckp->cop", table_mine, mine, preferred_element_type=jnp.float32)
        + jnp.einsum("ok,ckp->cop", table_other, other, preferred_element_type=jnp.float32)
    ).astype(jnp.bfloat16).reshape(columns, half_pixels)
    proj_wide = projection.astype(jnp.float32)
    power_part = jnp.sum(proj_wide * proj_wide, axis=1)
    cross_part = lax.dot_general(images, projection, (((1,), (1,)), ((), ())), preferred_element_type=jnp.float32)
    joint = cross_part - 0.5 * power_part[None, :]
    targets = jnp.arange(columns, dtype=jnp.int32)
    sel = jnp.sum(jnp.where(orient_lists[:, :, None] == targets[None, None, :], joint[:, None, :], 0.0), axis=2)
    sel = lax.psum(sel, "vol")
    score_scale = 4.0 / math.sqrt(half_pixels * halves)
    weights, log_norm = posterior(sel, offsets, counts, score_scale)
    spread = spread_weights(weights, orient_lists, columns)
    all_spread = lax.all_gather(spread, "ptcl", axis=0, tiled=True)
    sum_rows = lax.dot_general(
        all_spread, all_images, (((0,), (0,)), ((), ())), preferred_element_type=jnp.float32
    )
    totals = jnp.sum(all_spread.astype(jnp.float32), axis=0)
    new_ref = back_project(sum_rows.astype(jnp.bfloat16), totals, slice_table, classes)
    return (new_ref, log_norm)


def solution(mesh):
    placed = (
        P("groups", "vol", None),
        P(),
        P(("groups", "ptcl"), "vol"),
        P(("groups", "ptcl"), None),
        P(("groups", "ptcl"), None),
        P(("groups", "ptcl")),
    )
    return jax.shard_map(
        on_device,
        mesh=mesh,
        in_specs=placed,
        out_specs=(P("groups", None, "vol"), P(("groups", "ptcl"))),
        check_vma=False,
    )
```

```python
import functools
import math

import jax
import jax.numpy as jnp
from jax import lax
from jax.experimental import pallas as pl
from jax.experimental.pallas import tpu as pltpu
from jax.sharding import PartitionSpec as P

MESH = pl.DeviceIdType.MESH
UP, DOWN, SIDE = 0, 1, 2
VMEM_LIMIT = 56 * 1024 * 1024


def grid_of(members):
    return (4, 2) if members == 8 else (members, 1)


def pieces_of(rows, pairs):
    if pairs == 1 or rows % 16 or rows < 48:
        return [(0, rows)] if pairs == 1 else [(0, 0), (0, rows)]
    first = 16
    half = (rows - first) // 32 * 16
    return [(0, first), (first, rows - first - half), (rows - half, half)]


def gather_kernel(
    members, width, score_scale,
    slabs, table, images, padded, offsets, lists, counts,
    rows_out, totals_out, norm_out,
    own_slab, peer_slab, gathered, acc, joint, part, notes,
    own_sem, slab_send, slab_recv, part_send, part_recv, note_send, note_recv, send_sem, recv_sem,
):
    line, pairs = grid_of(members)
    me = lax.axis_index("ptcl")
    vol = lax.axis_index("vol")
    z, y = me // pairs, me % pairs
    classes, kz_dev, pixels = slabs.shape
    orients = table.shape[0]
    rows, half = images.shape
    slots = offsets.shape[0]
    shift = pixels - width

    barrier = pltpu.get_barrier_semaphore()
    for k in range(1, members):
        pl.semaphore_signal(barrier, inc=1, device_id={"ptcl": (me + k) % members}, device_id_type=MESH)
    pl.semaphore_signal(barrier, inc=1, device_id={"vol": 1 - vol}, device_id_type=MESH)

    own_copies = []
    for c in range(classes):
        copy = pltpu.make_async_copy(
            slabs.at[c, :, pl.ds(pl.multiple_of(vol * shift, 128), width)], own_slab.at[c], own_sem.at[c]
        )
        copy.start()
        own_copies.append(copy)
    pl.semaphore_wait(barrier, members)

    parts = pieces_of(rows, pairs)
    early = 0 if pairs == 2 else -1

    def hop(way, piece, origin, source):
        start, size = parts[piece]
        if way == SIDE:
            target = z * pairs + (1 - y)
        else:
            target = (z + (1 if way == UP else -1)) * pairs + y
            target = jnp.clip(target, 0, members - 1)
        return pltpu.make_async_remote_copy(
            src_ref=source.at[pl.ds(start, size), :],
            dst_ref=gathered.at[origin, pl.ds(start, size), :],
            send_sem=send_sem.at[way, piece, origin],
            recv_sem=recv_sem.at[piece, origin],
            device_id={"ptcl": target},
            device_id_type=MESH,
        )

    def arrived(piece, origin):
        start, size = parts[piece]
        spot = gathered.at[origin, pl.ds(start, size), :]
        pltpu.make_async_copy(spot, spot, recv_sem.at[piece, origin]).wait()

    def relay(way, piece, origin, source):
        @pl.when(z < line - 1 if way == UP else z > 0)
        def _():
            hop(way, piece, origin, source).start()

    slab_copies = []
    for c in range(classes):
        copy = pltpu.make_async_remote_copy(
            src_ref=slabs.at[c, :, pl.ds(pl.multiple_of((1 - vol) * shift, 128), width)],
            dst_ref=peer_slab.at[c],
            send_sem=slab_send.at[c],
            recv_sem=slab_recv.at[c],
            device_id={"vol": 1 - vol},
            device_id_type=MESH,
        )
        copy.start()
        slab_copies.append(copy)
    late = [p for p in range(len(parts)) if p != early]
    if pairs == 2:
        hop(SIDE, early, me, images).start()
    for p in late:
        for way in (UP, DOWN):
            relay(way, p, me, images)
        if pairs == 2:
            hop(SIDE, p, me, images).start()
    if pairs == 2:
        for way in (UP, DOWN):
            relay(way, early, me, images)
    gathered[me] = images[...]

    first = vol == 0
    low, high = table[:, :kz_dev], table[:, kz_dev:]
    table_own = jnp.where(first, low, high)
    table_peer = jnp.where(first, high, low)
    for c in range(classes):
        own_copies[c].wait()
        acc[pl.ds(c * orients, orients), :] = jnp.dot(
            table_own, own_slab[c], preferred_element_type=jnp.float32
        )
    twin = z * pairs + (1 - y)
    if pairs == 2:
        arrived(early, twin)
        for way in (UP, DOWN):
            relay(way, early, twin, gathered.at[twin])

    lane = lax.broadcasted_iota(jnp.int32, (orients, width), 1)
    skip = vol * (width - half)
    inside = (lane >= skip) & (lane < skip + half)
    for c in range(classes):
        slab_copies[c].wait_recv()
        value = acc[pl.ds(c * orients, orients), :] + jnp.dot(
            table_peer, peer_slab[c], preferred_element_type=jnp.float32
        )
        value = jnp.where(inside, value, 0.0).astype(jnp.bfloat16)
        wide = value.astype(jnp.float32)
        power = jnp.sum(wide * wide, axis=1, keepdims=True)
        cross = lax.dot_general(
            value, padded[...], (((1,), (1,)), ((), ())), preferred_element_type=jnp.float32
        )
        joint[pl.ds(c * orients, orients), :] = cross - 0.5 * power

    column = lax.broadcasted_iota(jnp.int32, (classes * orients, rows), 0)
    for s in range(slots):
        hit = column == lists[s : s + 1, :]
        part[0, s : s + 1, :] = jnp.sum(jnp.where(hit, joint[...], 0.0), axis=0, keepdims=True)
    part_copy = pltpu.make_async_remote_copy(
        src_ref=part.at[0],
        dst_ref=part.at[1],
        send_sem=part_send,
        recv_sem=part_recv,
        device_id={"vol": 1 - vol},
        device_id_type=MESH,
    )
    part_copy.start()

    def step(t):
        for way in (UP, DOWN):
            @pl.when(z - 1 - t >= 0 if way == UP else z + 1 + t < line)
            def _():
                far = (z - 1 - t if way == UP else z + 1 + t) * pairs
                for p in late:
                    arrived(p, far + y)
                    relay(way, p, far + y, gathered.at[far + y])
                    if pairs == 2:
                        hop(SIDE, p, far + y, gathered.at[far + y]).start()
                if pairs == 2:
                    for q in range(pairs):
                        arrived(early, far + q)
                        relay(way, early, far + q, gathered.at[far + q])

    def accumulate(origin, fresh=False):
        def block(b, carry):
            base = pl.multiple_of(b * orients, orients)
            target = lax.broadcasted_iota(jnp.int32, (orients, rows), 0) + base
            target = target.astype(jnp.float32)
            note = notes[origin]
            spread = jnp.zeros((orients, rows), jnp.float32)
            for s in range(slots):
                hit = target == note[slots + s : slots + s + 1, :]
                spread = spread + jnp.where(hit, note[s : s + 1, :], 0.0)
            spread = spread.astype(jnp.bfloat16)
            total = jnp.sum(spread.astype(jnp.float32), axis=1, keepdims=True)
            total = jnp.broadcast_to(total, (orients, totals_out.shape[1]))
            value = jnp.dot(spread, gathered[origin], preferred_element_type=jnp.float32)
            spot = pl.ds(base, orients)
            if fresh:
                totals_out[spot, :] = total
                acc[spot, :half] = value
            else:
                totals_out[spot, :] += total
                acc[spot, :half] += value
            return carry

        lax.fori_loop(0, classes, block, 0)

    def note_arrived(origin):
        pltpu.make_async_copy(notes.at[origin], notes.at[origin], note_recv.at[origin]).wait()

    step(0)

    part_copy.wait_recv()
    scores = score_scale * (part[0] + part[1]) + offsets[...]
    slot = lax.broadcasted_iota(jnp.int32, (slots, rows), 0)
    live = slot < counts[...]
    masked = jnp.where(live, scores, -1e30)
    top = jnp.max(masked, axis=0, keepdims=True)
    expon = jnp.where(live, jnp.exp(masked - top), 0.0)
    whole = jnp.sum(expon, axis=0, keepdims=True)
    norm_out[...] = top + jnp.log(whole)
    notes[me, :slots, :] = expon / whole
    notes[me, slots:, :] = lists[...].astype(jnp.float32)
    note_copies = []
    for k in range(1, members):
        copy = pltpu.make_async_remote_copy(
            src_ref=notes.at[me],
            dst_ref=notes.at[me],
            send_sem=note_send.at[k],
            recv_sem=note_recv.at[me],
            device_id={"ptcl": (me + k) % members},
            device_id_type=MESH,
        )
        copy.start()
        note_copies.append(copy)
    accumulate(me, fresh=True)

    def add_pair(origin):
        note_arrived(origin)
        accumulate(origin)

    def add_twin(origin):
        for p in late:
            arrived(p, origin)
        note_arrived(origin)
        accumulate(origin)

    def settle(t):
        for way in (UP, DOWN):
            @pl.when(z - 1 - t >= 0 if way == UP else z + 1 + t < line)
            def _():
                add_pair((z - 1 - t if way == UP else z + 1 + t) * pairs + y)

    def settle_twin(t):
        for way in (UP, DOWN):
            @pl.when(z - 1 - t >= 0 if way == UP else z + 1 + t < line)
            def _():
                add_twin((z - 1 - t if way == UP else z + 1 + t) * pairs + (1 - y))

    for t in range(1, line - 1):
        step(t)
        if t == 1 and pairs == 2:
            add_twin(twin)
        settle(t - 1)
        if pairs == 2 and t >= 2:
            settle_twin(t - 2)
    settle(line - 2)
    if pairs == 2:
        for t in range(max(0, line - 3), line - 1):
            settle_twin(t)
    for c in range(classes):
        spot = pl.ds(c * orients, orients)
        rows_out[spot, :] = acc[spot, :half].astype(jnp.bfloat16)

    for copy in slab_copies + [part_copy] + note_copies:
        copy.wait_send()

    for way in (UP, DOWN):
        @pl.when(z < line - 1 if way == UP else z > 0)
        def _():
            for t in range(-1, line - 1):
                origin_z = z - 1 - t if way == UP else z + 1 + t

                @pl.when(origin_z >= 0 if way == UP else origin_z < line)
                def _():
                    for p in late:
                        hop(way, p, origin_z * pairs + y, images).wait_send()
                    if pairs == 2:
                        for q in range(pairs):
                            hop(way, early, origin_z * pairs + q, images).wait_send()
    if pairs == 2:
        hop(SIDE, early, me, images).wait_send()
        for other in range(line):
            for p in late:
                hop(SIDE, p, other * pairs + y, images).wait_send()


def back_kernel(table, rows, totals, out):
    kernel = table[...].astype(jnp.float32)
    below = 1.0 + lax.dot_general(
        kernel * kernel,
        totals[...],
        (((0,), (0,)), ((), ())),
        precision=lax.Precision.HIGHEST,
        preferred_element_type=jnp.float32,
    )[:, :1]
    above = lax.dot_general(
        table[...], rows[...], (((0,), (0,)), ((), ())), preferred_element_type=jnp.float32
    )
    out[0] = (above / below).astype(jnp.bfloat16)


def on_device(reference_slabs, slice_table, images, offsets, orient_lists, counts):
    classes, kz_dev, pixels = reference_slabs.shape
    orients, planes = slice_table.shape
    columns = classes * orients
    rows, half = images.shape
    slots = offsets.shape[1]
    members = lax.axis_size("ptcl")
    line, pairs = grid_of(members)
    parts = pieces_of(rows, pairs)
    width = pixels - half // 128 * 128
    spare = width - half
    padded = jnp.where(
        lax.axis_index("vol") == 0,
        jnp.pad(images, ((0, 0), (0, spare))),
        jnp.pad(images, ((0, 0), (spare, 0))),
    )
    score_scale = 4.0 / math.sqrt(pixels)
    vmem = pl.BlockSpec(memory_space=pltpu.VMEM)
    dma = pltpu.SemaphoreType.DMA
    sum_rows, totals, log_norm = pl.pallas_call(
        functools.partial(gather_kernel, members, width, score_scale),
        out_shape=(
            jax.ShapeDtypeStruct((columns, half), jnp.bfloat16),
            jax.ShapeDtypeStruct((columns, 128), jnp.float32),
            jax.ShapeDtypeStruct((1, rows), jnp.float32),
        ),
        in_specs=[pl.BlockSpec(memory_space=pl.ANY)] + [vmem] * 6,
        out_specs=(vmem, vmem, vmem),
        scratch_shapes=[
            pltpu.VMEM((classes, kz_dev, width), jnp.bfloat16),
            pltpu.VMEM((classes, kz_dev, width), jnp.bfloat16),
            pltpu.VMEM((members, rows, half), jnp.bfloat16),
            pltpu.VMEM((columns, width), jnp.float32),
            pltpu.VMEM((columns, rows), jnp.float32),
            pltpu.VMEM((2, slots, rows), jnp.float32),
            pltpu.VMEM((members, 2 * slots, rows), jnp.float32),
            dma((classes,)),
            dma((classes,)),
            dma((classes,)),
            dma,
            dma,
            dma((members,)),
            dma((members,)),
            dma((3, len(parts), members)),
            dma((len(parts), members)),
        ],
        compiler_params=pltpu.CompilerParams(
            collective_id=0, has_side_effects=True, vmem_limit_bytes=VMEM_LIMIT
        ),
        name="gather_and_sum",
    )(reference_slabs, slice_table, images, padded, offsets.T, orient_lists.T, counts[None, :])
    new_ref = pl.pallas_call(
        back_kernel,
        grid=(classes,),
        out_shape=jax.ShapeDtypeStruct((classes, planes, half), jnp.bfloat16),
        in_specs=[
            pl.BlockSpec((orients, planes), lambda c: (0, 0)),
            pl.BlockSpec((orients, half), lambda c: (c, 0)),
            pl.BlockSpec((orients, 128), lambda c: (c, 0)),
        ],
        out_specs=pl.BlockSpec((1, planes, half), lambda c: (c, 0, 0)),
        compiler_params=pltpu.CompilerParams(vmem_limit_bytes=VMEM_LIMIT),
        name="back_project",
    )(slice_table, sum_rows, totals)
    return (new_ref, log_norm[0])


def solution(mesh):
    placed = (
        P("groups", "vol", None),
        P(),
        P(("groups", "ptcl"), "vol"),
        P(("groups", "ptcl"), None),
        P(("groups", "ptcl"), None),
        P(("groups", "ptcl")),
    )
    return jax.shard_map(
        on_device,
        mesh=mesh,
        in_specs=placed,
        out_specs=(P("groups", None, "vol"), P(("groups", "ptcl"))),
        check_vma=False,
    )
```

```python
import functools
import math

import jax
import jax.numpy as jnp
from jax import lax
from jax.experimental import pallas as pl
from jax.experimental.pallas import tpu as pltpu
from jax.sharding import PartitionSpec as P

MESH = pl.DeviceIdType.MESH
UP, DOWN, SIDE = 0, 1, 2
VMEM_LIMIT = 56 * 1024 * 1024


def grid_of(members):
    return (4, 2) if members == 8 else (members, 1)


def pieces_of(rows, pairs):
    if pairs == 1 or rows % 16 or rows < 48:
        return [(0, rows)] if pairs == 1 else [(0, 0), (0, rows)]
    first = 16
    half = (rows - first) // 32 * 16
    return [(0, first), (first, rows - first - half), (rows - half, half)]


def gather_kernel(
    members, width, score_scale,
    slabs, planes_table, images, offsets, lists, counts,
    rows_out, totals_out, norm_out,
    own_slab, peer_slab, flat, spans, padded, gathered, acc, joint, part, notes,
    own_sem, slab_send, slab_recv, part_send, part_recv, note_send, note_recv, send_sem, recv_sem,
):
    line, pairs = grid_of(members)
    me = lax.axis_index("ptcl")
    vol = lax.axis_index("vol")
    z, y = me // pairs, me % pairs
    kz_dev, classes, pixels = slabs.shape
    planes, orients = planes_table.shape
    rows, half = images.shape
    slots = offsets.shape[0]
    shift = pixels - width

    barrier = pltpu.get_barrier_semaphore()
    for k in range(1, members):
        pl.semaphore_signal(barrier, inc=1, device_id={"ptcl": (me + k) % members}, device_id_type=MESH)
    pl.semaphore_signal(barrier, inc=1, device_id={"vol": 1 - vol}, device_id_type=MESH)

    own_copy = pltpu.make_async_copy(
        slabs.at[:, :, pl.ds(pl.multiple_of(vol * shift, 128), width)], own_slab, own_sem
    )
    own_copy.start()
    pl.semaphore_wait(barrier, members)

    parts = pieces_of(rows, pairs)
    early = 0 if pairs == 2 else -1

    def hop(way, piece, origin, source):
        start, size = parts[piece]
        if way == SIDE:
            target = z * pairs + (1 - y)
        else:
            target = (z + (1 if way == UP else -1)) * pairs + y
            target = jnp.clip(target, 0, members - 1)
        return pltpu.make_async_remote_copy(
            src_ref=source.at[pl.ds(start, size), :],
            dst_ref=gathered.at[origin, pl.ds(start, size), :],
            send_sem=send_sem.at[way, piece, origin],
            recv_sem=recv_sem.at[piece, origin],
            device_id={"ptcl": target},
            device_id_type=MESH,
        )

    def arrived(piece, origin):
        start, size = parts[piece]
        spot = gathered.at[origin, pl.ds(start, size), :]
        pltpu.make_async_copy(spot, spot, recv_sem.at[piece, origin]).wait()

    def relay(way, piece, origin, source):
        @pl.when(z < line - 1 if way == UP else z > 0)
        def _():
            hop(way, piece, origin, source).start()

    slab_copy = pltpu.make_async_remote_copy(
        src_ref=slabs.at[:, :, pl.ds(pl.multiple_of((1 - vol) * shift, 128), width)],
        dst_ref=peer_slab,
        send_sem=slab_send,
        recv_sem=slab_recv,
        device_id={"vol": 1 - vol},
        device_id_type=MESH,
    )
    slab_copy.start()
    late = [p for p in range(len(parts)) if p != early]
    if pairs == 2:
        hop(SIDE, early, me, images).start()
    for p in late:
        for way in (UP, DOWN):
            relay(way, p, me, images)
        if pairs == 2:
            hop(SIDE, p, me, images).start()
    if pairs == 2:
        for way in (UP, DOWN):
            relay(way, early, me, images)
    gathered[me] = images[...]

    pair = lax.broadcasted_iota(jnp.int32, (planes, kz_dev * classes), 1)
    plane = lax.broadcasted_iota(jnp.int32, (planes, kz_dev * classes), 0)
    of_class = lax.broadcasted_iota(jnp.int32, (orients, kz_dev * classes), 1) % classes
    for side, which in enumerate((vol, 1 - vol)):
        pick = jnp.where(plane == pair // classes + which * kz_dev, 1.0, 0.0).astype(jnp.bfloat16)
        repeated = lax.dot_general(
            planes_table[...], pick, (((0,), (0,)), ((), ())), preferred_element_type=jnp.float32
        )
        for c in range(classes):
            spans[side, c * orients : (c + 1) * orients, :] = jnp.where(
                of_class == c, repeated, 0.0
            ).astype(jnp.bfloat16)

    @pl.when(vol == 0)
    def _():
        padded[:, :half] = images[...]
        padded[:, half:] = jnp.zeros((rows, width - half), jnp.bfloat16)

    @pl.when(vol != 0)
    def _():
        padded[:, width - half :] = images[...]
        padded[:, : width - half] = jnp.zeros((rows, width - half), jnp.bfloat16)

    own_copy.wait()
    flat[0] = own_slab[...].reshape(kz_dev * classes, width)
    twin = z * pairs + (1 - y)
    if pairs == 2:
        arrived(early, twin)
        for way in (UP, DOWN):
            relay(way, early, twin, gathered.at[twin])

    slab_copy.wait_recv()
    flat[1] = peer_slab[...].reshape(kz_dev * classes, width)
    skip = vol * (width - half)
    power = jnp.zeros((classes * orients, 1), jnp.float32)
    for start in range(0, width, 1024):
        size = min(1024, width - start)
        value = jnp.dot(spans[0], flat[0, :, start : start + size], preferred_element_type=jnp.float32)
        value = value + jnp.dot(
            spans[1], flat[1, :, start : start + size], preferred_element_type=jnp.float32
        )
        lane = lax.broadcasted_iota(jnp.int32, (classes * orients, size), 1) + start
        value = jnp.where((lane >= skip) & (lane < skip + half), value, 0.0).astype(jnp.bfloat16)
        wide = value.astype(jnp.float32)
        power = power + jnp.sum(wide * wide, axis=1, keepdims=True)
        cross = lax.dot_general(
            value,
            padded[:, start : start + size],
            (((1,), (1,)), ((), ())),
            preferred_element_type=jnp.float32,
        )
        if start == 0:
            joint[...] = cross
        else:
            joint[...] += cross
    joint[...] -= 0.5 * power

    column = lax.broadcasted_iota(jnp.int32, (classes * orients, rows), 0)
    for s in range(slots):
        hit = column == lists[s : s + 1, :]
        part[0, s : s + 1, :] = jnp.sum(jnp.where(hit, joint[...], 0.0), axis=0, keepdims=True)
    part_copy = pltpu.make_async_remote_copy(
        src_ref=part.at[0],
        dst_ref=part.at[1],
        send_sem=part_send,
        recv_sem=part_recv,
        device_id={"vol": 1 - vol},
        device_id_type=MESH,
    )
    part_copy.start()

    def step(t):
        for way in (UP, DOWN):
            @pl.when(z - 1 - t >= 0 if way == UP else z + 1 + t < line)
            def _():
                far = (z - 1 - t if way == UP else z + 1 + t) * pairs
                for p in late:
                    arrived(p, far + y)
                    relay(way, p, far + y, gathered.at[far + y])
                    if pairs == 2:
                        hop(SIDE, p, far + y, gathered.at[far + y]).start()
                if pairs == 2:
                    for q in range(pairs):
                        arrived(early, far + q)
                        relay(way, early, far + q, gathered.at[far + q])

    def accumulate(origin, fresh=False):
        def block(b, carry):
            base = pl.multiple_of(b * orients, orients)
            target = lax.broadcasted_iota(jnp.int32, (orients, rows), 0) + base
            target = target.astype(jnp.float32)
            note = notes[origin]
            spread = jnp.zeros((orients, rows), jnp.float32)
            for s in range(slots):
                hit = target == note[slots + s : slots + s + 1, :]
                spread = spread + jnp.where(hit, note[s : s + 1, :], 0.0)
            spread = spread.astype(jnp.bfloat16)
            total = jnp.sum(spread.astype(jnp.float32), axis=1, keepdims=True)
            total = jnp.broadcast_to(total, (orients, totals_out.shape[1]))
            value = jnp.dot(spread, gathered[origin], preferred_element_type=jnp.float32)
            spot = pl.ds(base, orients)
            if fresh:
                totals_out[spot, :] = total
                acc[spot, :half] = value
            else:
                totals_out[spot, :] += total
                acc[spot, :half] += value
            return carry

        lax.fori_loop(0, classes, block, 0)

    def note_arrived(origin):
        pltpu.make_async_copy(notes.at[origin], notes.at[origin], note_recv.at[origin]).wait()

    step(0)

    part_copy.wait_recv()
    scores = score_scale * (part[0] + part[1]) + offsets[...]
    slot = lax.broadcasted_iota(jnp.int32, (slots, rows), 0)
    live = slot < counts[...]
    masked = jnp.where(live, scores, -1e30)
    top = jnp.max(masked, axis=0, keepdims=True)
    expon = jnp.where(live, jnp.exp(masked - top), 0.0)
    whole = jnp.sum(expon, axis=0, keepdims=True)
    norm_out[...] = top + jnp.log(whole)
    notes[me, :slots, :] = expon / whole
    notes[me, slots:, :] = lists[...].astype(jnp.float32)
    note_copies = []
    for k in range(1, members):
        copy = pltpu.make_async_remote_copy(
            src_ref=notes.at[me],
            dst_ref=notes.at[me],
            send_sem=note_send.at[k],
            recv_sem=note_recv.at[me],
            device_id={"ptcl": (me + k) % members},
            device_id_type=MESH,
        )
        copy.start()
        note_copies.append(copy)
    accumulate(me, fresh=True)

    def add_pair(origin):
        note_arrived(origin)
        accumulate(origin)

    def add_twin(origin):
        for p in late:
            arrived(p, origin)
        note_arrived(origin)
        accumulate(origin)

    def settle(t):
        for way in (UP, DOWN):
            @pl.when(z - 1 - t >= 0 if way == UP else z + 1 + t < line)
            def _():
                add_pair((z - 1 - t if way == UP else z + 1 + t) * pairs + y)

    def settle_twin(t):
        for way in (UP, DOWN):
            @pl.when(z - 1 - t >= 0 if way == UP else z + 1 + t < line)
            def _():
                add_twin((z - 1 - t if way == UP else z + 1 + t) * pairs + (1 - y))

    for t in range(1, line - 1):
        step(t)
        if t == 1 and pairs == 2:
            add_twin(twin)
        settle(t - 1)
        if pairs == 2 and t >= 2:
            settle_twin(t - 2)
    settle(line - 2)
    if pairs == 2:
        for t in range(max(0, line - 3), line - 1):
            settle_twin(t)
    for c in range(classes):
        spot = pl.ds(c * orients, orients)
        rows_out[spot, :] = acc[spot, :half].astype(jnp.bfloat16)

    for copy in [slab_copy, part_copy] + note_copies:
        copy.wait_send()

    for way in (UP, DOWN):
        @pl.when(z < line - 1 if way == UP else z > 0)
        def _():
            for t in range(-1, line - 1):
                origin_z = z - 1 - t if way == UP else z + 1 + t

                @pl.when(origin_z >= 0 if way == UP else origin_z < line)
                def _():
                    for p in late:
                        hop(way, p, origin_z * pairs + y, images).wait_send()
                    if pairs == 2:
                        for q in range(pairs):
                            hop(way, early, origin_z * pairs + q, images).wait_send()
    if pairs == 2:
        hop(SIDE, early, me, images).wait_send()
        for other in range(line):
            for p in late:
                hop(SIDE, p, other * pairs + y, images).wait_send()


def back_kernel(planes_table, rows, totals, out):
    part, classes, half = out.shape
    planes, orients = planes_table.shape
    pair = lax.broadcasted_iota(jnp.int32, (part * classes, planes), 0)
    plane = lax.broadcasted_iota(jnp.int32, (part * classes, planes), 1)
    pick = jnp.where(plane == pair // classes + pl.program_id(0) * part, 1.0, 0.0).astype(jnp.bfloat16)
    repeated = jnp.dot(pick, planes_table[...], preferred_element_type=jnp.float32)
    of_class = lax.broadcasted_iota(jnp.int32, (part * classes, orients), 0) % classes
    blocks = []
    below = 1.0
    for c in range(classes):
        block = jnp.where(of_class == c, repeated, 0.0)
        below = below + jnp.dot(
            block * block,
            totals[c * orients : (c + 1) * orients, :],
            precision=lax.Precision.HIGHEST,
            preferred_element_type=jnp.float32,
        )
        blocks.append(block.astype(jnp.bfloat16))
    above = jnp.dot(jnp.concatenate(blocks, axis=1), rows[...], preferred_element_type=jnp.float32)
    out[...] = (above / below[:, :1]).astype(jnp.bfloat16).reshape(part, classes, half)


def on_device(reference_slabs, slice_table, images, offsets, orient_lists, counts):
    classes, kz_dev, pixels = reference_slabs.shape
    orients, planes = slice_table.shape
    columns = classes * orients
    rows, half = images.shape
    slots = offsets.shape[1]
    members = lax.axis_size("ptcl")
    line, pairs = grid_of(members)
    parts = pieces_of(rows, pairs)
    width = pixels - half // 128 * 128
    planes_table = slice_table.T
    part = max(d for d in range(1, planes + 1) if planes % d == 0 and (d == planes or d * classes % 16 == 0 and d <= 40))
    score_scale = 4.0 / math.sqrt(pixels)
    vmem = pl.BlockSpec(memory_space=pltpu.VMEM)
    dma = pltpu.SemaphoreType.DMA
    sum_rows, totals, log_norm = pl.pallas_call(
        functools.partial(gather_kernel, members, width, score_scale),
        out_shape=(
            jax.ShapeDtypeStruct((columns, half), jnp.bfloat16),
            jax.ShapeDtypeStruct((columns, 128), jnp.float32),
            jax.ShapeDtypeStruct((1, rows), jnp.float32),
        ),
        in_specs=[pl.BlockSpec(memory_space=pl.ANY)] + [vmem] * 5,
        out_specs=(vmem, vmem, vmem),
        scratch_shapes=[
            pltpu.VMEM((kz_dev, classes, width), jnp.bfloat16),
            pltpu.VMEM((kz_dev, classes, width), jnp.bfloat16),
            pltpu.VMEM((2, kz_dev * classes, width), jnp.bfloat16),
            pltpu.VMEM((2, columns, kz_dev * classes), jnp.bfloat16),
            pltpu.VMEM((rows, width), jnp.bfloat16),
            pltpu.VMEM((members, rows, half), jnp.bfloat16),
            pltpu.VMEM((columns, half), jnp.float32),
            pltpu.VMEM((columns, rows), jnp.float32),
            pltpu.VMEM((2, slots, rows), jnp.float32),
            pltpu.VMEM((members, 2 * slots, rows), jnp.float32),
            dma,
            dma,
            dma,
            dma,
            dma,
            dma((members,)),
            dma((members,)),
            dma((3, len(parts), members)),
            dma((len(parts), members)),
        ],
        compiler_params=pltpu.CompilerParams(
            collective_id=0, has_side_effects=True, vmem_limit_bytes=VMEM_LIMIT
        ),
        name="gather_and_sum",
    )(
        jnp.swapaxes(reference_slabs, 0, 1), planes_table, images, offsets.T, orient_lists.T, counts[None, :]
    )
    new_ref = pl.pallas_call(
        back_kernel,
        grid=(planes // part,),
        out_shape=jax.ShapeDtypeStruct((planes, classes, half), jnp.bfloat16),
        in_specs=[vmem, vmem, vmem],
        out_specs=pl.BlockSpec((part, classes, half), lambda b: (b, 0, 0)),
        compiler_params=pltpu.CompilerParams(vmem_limit_bytes=VMEM_LIMIT),
        name="back_project",
    )(planes_table, sum_rows, totals)
    return (jnp.swapaxes(new_ref, 0, 1), log_norm[0])


def solution(mesh):
    placed = (
        P("groups", "vol", None),
        P(),
        P(("groups", "ptcl"), "vol"),
        P(("groups", "ptcl"), None),
        P(("groups", "ptcl"), None),
        P(("groups", "ptcl")),
    )
    return jax.shard_map(
        on_device,
        mesh=mesh,
        in_specs=placed,
        out_specs=(P("groups", None, "vol"), P(("groups", "ptcl"))),
        check_vma=False,
    )
```

```python
import functools
import math

import jax
import jax.numpy as jnp
from jax import lax
from jax.experimental import pallas as pl
from jax.experimental.pallas import tpu as pltpu
from jax.sharding import PartitionSpec as P

MESH = pl.DeviceIdType.MESH
UP, DOWN, SIDE = 0, 1, 2
VMEM_LIMIT = 56 * 1024 * 1024


def grid_of(members):
    return (4, 2) if members == 8 else (members, 1)


def pieces_of(rows, pairs):
    if pairs == 1 or rows % 16 or rows < 48:
        return [(0, rows)] if pairs == 1 else [(0, 0), (0, rows)]
    first = 16
    return [(0, first)] + [(at, min(32, rows - at)) for at in range(first, rows, 32)]


def gather_kernel(
    members, width, score_scale,
    slabs, planes_table, images, offsets, lists, counts,
    rows_out, totals_out, norm_out,
    own_slab, peer_slab, flat, spans, padded, gathered, acc, joint, part, notes,
    own_sem, slab_send, slab_recv, part_send, part_recv, note_send, note_recv, send_sem, recv_sem,
):
    line, pairs = grid_of(members)
    me = lax.axis_index("ptcl")
    vol = lax.axis_index("vol")
    z, y = me // pairs, me % pairs
    kz_dev, classes, pixels = slabs.shape
    planes, orients = planes_table.shape
    rows, half = images.shape
    slots = offsets.shape[0]
    shift = pixels - width

    barrier = pltpu.get_barrier_semaphore()
    for k in range(1, members):
        pl.semaphore_signal(barrier, inc=1, device_id={"ptcl": (me + k) % members}, device_id_type=MESH)
    pl.semaphore_signal(barrier, inc=1, device_id={"vol": 1 - vol}, device_id_type=MESH)

    own_copy = pltpu.make_async_copy(
        slabs.at[:, :, pl.ds(pl.multiple_of(vol * shift, 128), width)], own_slab, own_sem
    )
    own_copy.start()
    pl.semaphore_wait(barrier, members)

    parts = pieces_of(rows, pairs)
    early = 0 if pairs == 2 else -1

    def hop(way, piece, origin, source):
        start, size = parts[piece]
        if way == SIDE:
            target = z * pairs + (1 - y)
        else:
            target = (z + (1 if way == UP else -1)) * pairs + y
            target = jnp.clip(target, 0, members - 1)
        return pltpu.make_async_remote_copy(
            src_ref=source.at[pl.ds(start, size), :],
            dst_ref=gathered.at[origin, pl.ds(start, size), :],
            send_sem=send_sem.at[way, piece, origin],
            recv_sem=recv_sem.at[piece, origin],
            device_id={"ptcl": target},
            device_id_type=MESH,
        )

    def arrived(piece, origin):
        start, size = parts[piece]
        spot = gathered.at[origin, pl.ds(start, size), :]
        pltpu.make_async_copy(spot, spot, recv_sem.at[piece, origin]).wait()

    def relay(way, piece, origin, source):
        @pl.when(z < line - 1 if way == UP else z > 0)
        def _():
            hop(way, piece, origin, source).start()

    slab_copy = pltpu.make_async_remote_copy(
        src_ref=slabs.at[:, :, pl.ds(pl.multiple_of((1 - vol) * shift, 128), width)],
        dst_ref=peer_slab,
        send_sem=slab_send,
        recv_sem=slab_recv,
        device_id={"vol": 1 - vol},
        device_id_type=MESH,
    )
    slab_copy.start()
    late = [p for p in range(len(parts)) if p != early]
    if pairs == 2:
        hop(SIDE, early, me, images).start()
    for p in late:
        for way in (UP, DOWN):
            relay(way, p, me, images)
        if pairs == 2:
            hop(SIDE, p, me, images).start()
    if pairs == 2:
        for way in (UP, DOWN):
            relay(way, early, me, images)
    gathered[me] = images[...]

    pair = lax.broadcasted_iota(jnp.int32, (planes, kz_dev * classes), 1)
    plane = lax.broadcasted_iota(jnp.int32, (planes, kz_dev * classes), 0)
    of_class = lax.broadcasted_iota(jnp.int32, (orients, kz_dev * classes), 1) % classes
    for side, which in enumerate((vol, 1 - vol)):
        pick = jnp.where(plane == pair // classes + which * kz_dev, 1.0, 0.0).astype(jnp.bfloat16)
        repeated = lax.dot_general(
            planes_table[...], pick, (((0,), (0,)), ((), ())), preferred_element_type=jnp.float32
        )
        for c in range(classes):
            spans[side, c * orients : (c + 1) * orients, :] = jnp.where(
                of_class == c, repeated, 0.0
            ).astype(jnp.bfloat16)

    @pl.when(vol == 0)
    def _():
        padded[:, :half] = images[...]
        padded[:, half:] = jnp.zeros((rows, width - half), jnp.bfloat16)

    @pl.when(vol != 0)
    def _():
        padded[:, width - half :] = images[...]
        padded[:, : width - half] = jnp.zeros((rows, width - half), jnp.bfloat16)

    own_copy.wait()
    flat[0] = own_slab[...].reshape(kz_dev * classes, width)
    twin = z * pairs + (1 - y)
    if pairs == 2:
        arrived(early, twin)
        for way in (UP, DOWN):
            relay(way, early, twin, gathered.at[twin])

    slab_copy.wait_recv()
    flat[1] = peer_slab[...].reshape(kz_dev * classes, width)
    skip = vol * (width - half)
    power = jnp.zeros((classes * orients, 1), jnp.float32)
    for start in range(0, width, 1024):
        size = min(1024, width - start)
        value = jnp.dot(spans[0], flat[0, :, start : start + size], preferred_element_type=jnp.float32)
        value = value + jnp.dot(
            spans[1], flat[1, :, start : start + size], preferred_element_type=jnp.float32
        )
        lane = lax.broadcasted_iota(jnp.int32, (classes * orients, size), 1) + start
        value = jnp.where((lane >= skip) & (lane < skip + half), value, 0.0).astype(jnp.bfloat16)
        wide = value.astype(jnp.float32)
        power = power + jnp.sum(wide * wide, axis=1, keepdims=True)
        cross = lax.dot_general(
            value,
            padded[:, start : start + size],
            (((1,), (1,)), ((), ())),
            preferred_element_type=jnp.float32,
        )
        if start == 0:
            joint[...] = cross
        else:
            joint[...] += cross
    joint[...] -= 0.5 * power

    column = lax.broadcasted_iota(jnp.int32, (classes * orients, rows), 0)
    for s in range(slots):
        hit = column == lists[s : s + 1, :]
        part[0, s : s + 1, :] = jnp.sum(jnp.where(hit, joint[...], 0.0), axis=0, keepdims=True)
    part_copy = pltpu.make_async_remote_copy(
        src_ref=part.at[0],
        dst_ref=part.at[1],
        send_sem=part_send,
        recv_sem=part_recv,
        device_id={"vol": 1 - vol},
        device_id_type=MESH,
    )
    part_copy.start()

    def step(t):
        for p in late:
            for way in (UP, DOWN):
                @pl.when(z - 1 - t >= 0 if way == UP else z + 1 + t < line)
                def _():
                    far = (z - 1 - t if way == UP else z + 1 + t) * pairs
                    arrived(p, far + y)
                    relay(way, p, far + y, gathered.at[far + y])
                    if pairs == 2:
                        hop(SIDE, p, far + y, gathered.at[far + y]).start()
        if pairs == 2:
            for way in (UP, DOWN):
                @pl.when(z - 1 - t >= 0 if way == UP else z + 1 + t < line)
                def _():
                    far = (z - 1 - t if way == UP else z + 1 + t) * pairs
                    for q in range(pairs):
                        arrived(early, far + q)
                        relay(way, early, far + q, gathered.at[far + q])

    def accumulate(origin, fresh=False):
        def block(b, carry):
            base = pl.multiple_of(b * orients, orients)
            target = lax.broadcasted_iota(jnp.int32, (orients, rows), 0) + base
            target = target.astype(jnp.float32)
            note = notes[origin]
            spread = jnp.zeros((orients, rows), jnp.float32)
            for s in range(slots):
                hit = target == note[slots + s : slots + s + 1, :]
                spread = spread + jnp.where(hit, note[s : s + 1, :], 0.0)
            spread = spread.astype(jnp.bfloat16)
            total = jnp.sum(spread.astype(jnp.float32), axis=1, keepdims=True)
            total = jnp.broadcast_to(total, (orients, totals_out.shape[1]))
            value = jnp.dot(spread, gathered[origin], preferred_element_type=jnp.float32)
            spot = pl.ds(base, orients)
            if fresh:
                totals_out[spot, :] = total
                acc[spot, :half] = value
            else:
                totals_out[spot, :] += total
                acc[spot, :half] += value
            return carry

        lax.fori_loop(0, classes, block, 0)

    def note_arrived(origin):
        pltpu.make_async_copy(notes.at[origin], notes.at[origin], note_recv.at[origin]).wait()

    step(0)

    part_copy.wait_recv()
    scores = score_scale * (part[0] + part[1]) + offsets[...]
    slot = lax.broadcasted_iota(jnp.int32, (slots, rows), 0)
    live = slot < counts[...]
    masked = jnp.where(live, scores, -1e30)
    top = jnp.max(masked, axis=0, keepdims=True)
    expon = jnp.where(live, jnp.exp(masked - top), 0.0)
    whole = jnp.sum(expon, axis=0, keepdims=True)
    norm_out[...] = top + jnp.log(whole)
    notes[me, :slots, :] = expon / whole
    notes[me, slots:, :] = lists[...].astype(jnp.float32)
    note_copies = []
    for k in range(1, members):
        copy = pltpu.make_async_remote_copy(
            src_ref=notes.at[me],
            dst_ref=notes.at[me],
            send_sem=note_send.at[k],
            recv_sem=note_recv.at[me],
            device_id={"ptcl": (me + k) % members},
            device_id_type=MESH,
        )
        copy.start()
        note_copies.append(copy)
    accumulate(me, fresh=True)

    def add_pair(origin):
        note_arrived(origin)
        accumulate(origin)

    def add_twin(origin):
        for p in late:
            arrived(p, origin)
        note_arrived(origin)
        accumulate(origin)

    def settle(t):
        for way in (UP, DOWN):
            @pl.when(z - 1 - t >= 0 if way == UP else z + 1 + t < line)
            def _():
                add_pair((z - 1 - t if way == UP else z + 1 + t) * pairs + y)

    def settle_twin(t):
        for way in (UP, DOWN):
            @pl.when(z - 1 - t >= 0 if way == UP else z + 1 + t < line)
            def _():
                add_twin((z - 1 - t if way == UP else z + 1 + t) * pairs + (1 - y))

    for t in range(1, line - 1):
        step(t)
        if t == 1 and pairs == 2:
            add_twin(twin)
        settle(t - 1)
        if pairs == 2 and t >= 2:
            settle_twin(t - 2)
    settle(line - 2)
    if pairs == 2:
        for t in range(max(0, line - 3), line - 1):
            settle_twin(t)
    for c in range(classes):
        spot = pl.ds(c * orients, orients)
        rows_out[spot, :] = acc[spot, :half].astype(jnp.bfloat16)

    for copy in [slab_copy, part_copy] + note_copies:
        copy.wait_send()

    for way in (UP, DOWN):
        @pl.when(z < line - 1 if way == UP else z > 0)
        def _():
            for t in range(-1, line - 1):
                origin_z = z - 1 - t if way == UP else z + 1 + t

                @pl.when(origin_z >= 0 if way == UP else origin_z < line)
                def _():
                    for p in late:
                        hop(way, p, origin_z * pairs + y, images).wait_send()
                    if pairs == 2:
                        for q in range(pairs):
                            hop(way, early, origin_z * pairs + q, images).wait_send()
    if pairs == 2:
        hop(SIDE, early, me, images).wait_send()
        for other in range(line):
            for p in late:
                hop(SIDE, p, other * pairs + y, images).wait_send()


def back_kernel(planes_table, rows, totals, out):
    part, classes, half = out.shape
    planes, orients = planes_table.shape
    pair = lax.broadcasted_iota(jnp.int32, (part * classes, planes), 0)
    plane = lax.broadcasted_iota(jnp.int32, (part * classes, planes), 1)
    pick = jnp.where(plane == pair // classes + pl.program_id(0) * part, 1.0, 0.0).astype(jnp.bfloat16)
    repeated = jnp.dot(pick, planes_table[...], preferred_element_type=jnp.float32)
    of_class = lax.broadcasted_iota(jnp.int32, (part * classes, orients), 0) % classes
    blocks = []
    below = 1.0
    for c in range(classes):
        block = jnp.where(of_class == c, repeated, 0.0)
        below = below + jnp.dot(
            block * block,
            totals[c * orients : (c + 1) * orients, :],
            precision=lax.Precision.HIGHEST,
            preferred_element_type=jnp.float32,
        )
        blocks.append(block.astype(jnp.bfloat16))
    above = jnp.dot(jnp.concatenate(blocks, axis=1), rows[...], preferred_element_type=jnp.float32)
    out[...] = (above / below[:, :1]).astype(jnp.bfloat16).reshape(part, classes, half)


def on_device(reference_slabs, slice_table, images, offsets, orient_lists, counts):
    classes, kz_dev, pixels = reference_slabs.shape
    orients, planes = slice_table.shape
    columns = classes * orients
    rows, half = images.shape
    slots = offsets.shape[1]
    members = lax.axis_size("ptcl")
    line, pairs = grid_of(members)
    parts = pieces_of(rows, pairs)
    width = pixels - half // 128 * 128
    planes_table = slice_table.T
    part = max(d for d in range(1, planes + 1) if planes % d == 0 and (d == planes or d * classes % 16 == 0 and d <= 60))
    score_scale = 4.0 / math.sqrt(pixels)
    vmem = pl.BlockSpec(memory_space=pltpu.VMEM)
    dma = pltpu.SemaphoreType.DMA
    sum_rows, totals, log_norm = pl.pallas_call(
        functools.partial(gather_kernel, members, width, score_scale),
        out_shape=(
            jax.ShapeDtypeStruct((columns, half), jnp.bfloat16),
            jax.ShapeDtypeStruct((columns, 128), jnp.float32),
            jax.ShapeDtypeStruct((1, rows), jnp.float32),
        ),
        in_specs=[pl.BlockSpec(memory_space=pl.ANY)] + [vmem] * 5,
        out_specs=(vmem, vmem, vmem),
        scratch_shapes=[
            pltpu.VMEM((kz_dev, classes, width), jnp.bfloat16),
            pltpu.VMEM((kz_dev, classes, width), jnp.bfloat16),
            pltpu.VMEM((2, kz_dev * classes, width), jnp.bfloat16),
            pltpu.VMEM((2, columns, kz_dev * classes), jnp.bfloat16),
            pltpu.VMEM((rows, width), jnp.bfloat16),
            pltpu.VMEM((members, rows, half), jnp.bfloat16),
            pltpu.VMEM((columns, half), jnp.float32),
            pltpu.VMEM((columns, rows), jnp.float32),
            pltpu.VMEM((2, slots, rows), jnp.float32),
            pltpu.VMEM((members, 2 * slots, rows), jnp.float32),
            dma,
            dma,
            dma,
            dma,
            dma,
            dma((members,)),
            dma((members,)),
            dma((3, len(parts), members)),
            dma((len(parts), members)),
        ],
        compiler_params=pltpu.CompilerParams(
            collective_id=0, has_side_effects=True, vmem_limit_bytes=VMEM_LIMIT
        ),
        name="gather_and_sum",
    )(
        jnp.swapaxes(reference_slabs, 0, 1), planes_table, images, offsets.T, orient_lists.T, counts[None, :]
    )
    new_ref = pl.pallas_call(
        back_kernel,
        grid=(planes // part,),
        out_shape=jax.ShapeDtypeStruct((planes, classes, half), jnp.bfloat16),
        in_specs=[vmem, vmem, vmem],
        out_specs=pl.BlockSpec((part, classes, half), lambda b: (b, 0, 0)),
        compiler_params=pltpu.CompilerParams(vmem_limit_bytes=VMEM_LIMIT),
        name="back_project",
    )(planes_table, sum_rows, totals)
    return (jnp.swapaxes(new_ref, 0, 1), log_norm[0])


def solution(mesh):
    placed = (
        P("groups", "vol", None),
        P(),
        P(("groups", "ptcl"), "vol"),
        P(("groups", "ptcl"), None),
        P(("groups", "ptcl"), None),
        P(("groups", "ptcl")),
    )
    return jax.shard_map(
        on_device,
        mesh=mesh,
        in_specs=placed,
        out_specs=(P("groups", None, "vol"), P(("groups", "ptcl"))),
        check_vma=False,
    )
```
